512 devices in a mesh: seq: 64 (over y, z), head: 8 (over x, core).
Axes of the slice: x: 4, y: 4, z: 16, core: 2. Of those that a mesh axis runs over, the one named last changes fastest.
Arguments:
- query_vec: bfloat16 [65536, 2048], P('seq', 'head'), may hold values from -6 to 6
- key_vec: bfloat16 [65536, 2048], P('seq', 'head'), may hold values from -6 to 6
- value_vec: bfloat16 [65536, 2048], P('seq', 'head'), may hold values from -60 to 60
- cotangent: bfloat16 [65536, 2048], P('seq', 'head'), may hold values from -6 to 6
- norm_gain: float32 [2048], P('head'), may hold values from 0.5 to 1.5
- doc_ids: int32 [65536], P('seq'), may hold values from 0 to 63, never falling along the last dimension, each value on 1 to 4096 neighbouring positions
- lang_ids: int32 [65536], P('seq'), may hold values from 0 to 15
- loss_table: float32 [16], replicated, may hold values from 0.25 to 4
Outputs:
- grad_query: bfloat16 [65536, 2048], P('seq', 'head')
- grad_key: bfloat16 [65536, 2048], P('seq', 'head')
- grad_value: bfloat16 [65536, 2048], P('seq', 'head')
The draws below stay inside these ranges and needn't reach their ends.
Inputs may be any that keep to these rules, and one draw needn't show every extreme that they name: `doc_ids`: document numbers never fall along the row, each of 0 to 63 occurs, every document has 1 to 4096 tokens and one has exactly 4096.
All inputs are finite; a program needn't handle non-finite values.
Results may differ from the reference program's by a relative error of at most 0.0058.
Values sent between devices are 32-bit elements; how exact they have to be, the bound alone decides.
No kernel may reach another device: no remote copies, remote signals or barrier semaphores. Data moves between devices by JAX's collectives and lax.ppermute only.
A program may use at most 64 MiB of HBM per device.

```python
import math
import jax
import jax.numpy as jnp
import numpy as np
from jax import lax

HEAD_DIM = 128
HEADS = 16
TOK_DEV = 1024
NLANG = 16
TOKENS = 65536
DOCS = 64
DOC_MOST = 4096


def draw_value_vec(key, part):
    key_base, key_rough = jax.random.split(key, 2)
    columns = HEADS * HEAD_DIM
    ramp = jnp.arange(columns, dtype=jnp.float32) / (columns - 1)
    base = jnp.clip(jax.random.normal(key_base, (TOKENS, columns), jnp.float32), -6.0, 6.0)
    slope = math.log(3.0)
    rough = jnp.exp(jax.random.uniform(key_rough, (columns,), jnp.float32, 0.0, math.log(3.3)))
    return (base * jnp.exp(slope * ramp)[None, :] * rough[None, :]).astype(jnp.bfloat16)


def plant(values, rng, low, top_value):
    longest = values.shape.index(max(values.shape))
    spots = []
    for shift in (0, 1):
        where = [jax.random.randint(jax.random.fold_in(rng, axis), (), 0, length) for axis, length in enumerate(values.shape)]
        where[longest] = (where[longest] + shift) % values.shape[longest]
        spots.append(tuple(where))
    return values.at[spots[0]].set(low).at[spots[1]].set(top_value)


def level_of(own_key, extent, pieces, smallest, largest):
    def one(dim, parts):
        steps = jax.random.uniform(jax.random.fold_in(jax.random.fold_in(own_key, 6), dim), (parts,), jnp.float32, smallest / len(pieces), largest / len(pieces))
        return jnp.repeat(jnp.exp(steps), extent[dim] // parts).reshape((-1,) + (1,) * (len(extent) - dim - 1))

    gain = one(*pieces[0])
    for cut in pieces[1:]:
        gain = gain * one(*cut)
    return gain


def profile(amount, total, reach, skew):
    portions = [(1 << 20) // math.isqrt(standing ** skew) + 1 for standing in range(2, amount + 1)]
    rest, holding = total - reach - (amount - 1), [1] * (amount - 1)
    while rest > 0:
        free = [i for i in range(amount - 1) if holding[i] < reach]
        whole, remaining = sum([portions[i] for i in free]), rest
        for i in free:
            addition = min(reach - holding[i], max(1, remaining * portions[i] // whole), rest)
            holding[i] = holding[i] + addition
            rest = rest - addition
    return np.array([reach] + holding)


def ragged(stream_key, amount, total, limit, lean):
    if amount == 2:
        one = jax.random.randint(stream_key, (), max(1, total - limit), min(limit, total - 1) + 1)
        return jnp.stack([one, total - one])
    sizes = jnp.asarray(profile(amount, total, limit, lean), jnp.int32)
    twos = (amount - 1) // 2
    source_of, taker = sizes[1:1 + 2 * twos:2], sizes[2:2 + 2 * twos:2]
    room = jnp.minimum(source_of - 1, limit - taker)
    shifted = jax.random.randint(jax.random.fold_in(stream_key, 1), (twos,), 0, 1 << 20) % (room + 1)
    sizes = sizes.at[1:1 + 2 * twos:2].set(source_of - shifted).at[2:2 + 2 * twos:2].set(taker + shifted)
    return sizes[jax.random.permutation(jax.random.fold_in(stream_key, 2), amount)]


def centred(rng, shape, scale, reach, shards=(), kind=jnp.bfloat16):
    values = jax.random.normal(rng, shape, jnp.float32) * scale
    if len(shards) > 0:
        values = level_of(rng, shape, shards, -0.22, 0.18) * values
    return jnp.clip(values, min=-reach, max=reach).astype(kind)


def setup_inputs(seed: int = 0) -> dict:
    key_list = jax.random.split(jax.random.key(seed), 9)
    return {
        "query_vec": centred(key_list[0], (TOKENS, HEADS * HEAD_DIM), 1.0, 6.0, ((0, 64), (1, 8))),
        "key_vec": centred(key_list[1], (TOKENS, HEADS * HEAD_DIM), 1.0, 6.0, ((0, 64), (1, 8))),
        "value_vec": draw_value_vec(jax.random.fold_in(key_list[8], 71), 0),
        "cotangent": centred(key_list[3], (TOKENS, HEADS * HEAD_DIM), 1.0, 6.0, ((0, 64), (1, 8))),
        "norm_gain": jnp.clip(0.5 + 1.0 * jax.random.uniform(key_list[4], (HEADS * HEAD_DIM,), jnp.float32) ** level_of(key_list[4], (HEADS * HEAD_DIM,), ((0, 8),), -0.2, 0.2), 0.5, 1.5),
        "doc_ids": jnp.searchsorted(jnp.cumsum(ragged(key_list[5], DOCS, TOKENS, DOC_MOST, 2)), jnp.arange(TOKENS), side="right").astype(jnp.int32),
        "lang_ids": plant(jax.random.randint(key_list[6], (TOKENS,), 0, NLANG), jax.random.fold_in(key_list[6], 1), 0, NLANG - 1).astype(jnp.int32),
        "loss_table": jnp.clip(jnp.exp(jax.random.uniform(key_list[7], (NLANG,), jnp.float32, math.log(0.25), math.log(4.0))), 0.25, 4.0),
    }


EPSILON = 1e-06

def rounded(tensor):
    return lax.optimization_barrier(tensor.astype(jnp.bfloat16)).astype(jnp.float32)

def as_float(tensor):
    return tensor.astype(jnp.float32)

def visible_mask(doc_block):
    position = jnp.arange(doc_block.shape[0])
    causal = position[:, None] >= position[None, :]
    return causal & (doc_block[:, None] == doc_block[None, :])

def block_scores(query_blk, key_blk, doc_block):
    raw_scores = jnp.einsum('the,she->hts', as_float(query_blk), as_float(key_blk))
    return rounded(jnp.where(visible_mask(doc_block)[None], raw_scores, 0.0))

def forward_state(inputs):
    key_blk, value_blk, doc_block = inputs
    kept_keys = jnp.where((doc_block == doc_block[-1])[:, None, None], as_float(key_blk), 0.0)
    return jnp.einsum('the,thf->hef', kept_keys, as_float(value_blk))

def backward_state(inputs):
    query_blk, grad_blk, doc_block = inputs
    kept_queries = jnp.where((doc_block == doc_block[0])[:, None, None], as_float(query_blk), 0.0)
    return jnp.einsum('the,thf->hef', kept_queries, as_float(grad_blk))

def head_block(inputs):
    query_blk, key_blk, value_blk, doc_block, incoming_blk = inputs
    scores = block_scores(query_blk, key_blk, doc_block)
    inner = jnp.einsum('hts,shf->thf', scores, as_float(value_blk))
    carried = jnp.einsum('the,hef->thf', as_float(query_blk), incoming_blk)
    in_first = (doc_block == doc_block[0])[:, None, None]
    return inner + jnp.where(in_first, carried, 0.0)

def grad_block(inputs):
    query_blk, key_blk, value_blk, grad_blk, doc_block, incoming_blk, returning_blk = inputs
    query_f = as_float(query_blk)
    key_f = as_float(key_blk)
    value_f = as_float(value_blk)
    grad_f = as_float(grad_blk)
    scores = block_scores(query_blk, key_blk, doc_block)
    grad_raw = jnp.einsum('thf,shf->hts', grad_f, value_f)
    grad_scores = rounded(jnp.where(visible_mask(doc_block)[None], grad_raw, 0.0))
    in_first = (doc_block == doc_block[0])[:, None, None]
    in_last = (doc_block == doc_block[-1])[:, None, None]
    grad_q = jnp.einsum('hts,she->the', grad_scores, key_f) + jnp.where(in_first, jnp.einsum('thf,hef->the', grad_f, incoming_blk), 0.0)
    grad_k = jnp.einsum('hts,the->she', grad_scores, query_f) + jnp.where(in_last, jnp.einsum('shf,hef->she', value_f, returning_blk), 0.0)
    grad_v = jnp.einsum('hts,thf->shf', scores, grad_f) + jnp.where(in_last, jnp.einsum('she,hef->shf', key_f, returning_blk), 0.0)
    return (grad_q.astype(jnp.bfloat16), grad_k.astype(jnp.bfloat16), grad_v.astype(jnp.bfloat16))

def carry_forward(carry, inputs):
    running, prev_last = carry
    state_blk, first_doc, last_doc = inputs
    incoming = jnp.where(prev_last == first_doc, running, 0.0)
    running = state_blk + jnp.where(prev_last == last_doc, running, 0.0)
    return ((running, last_doc), incoming)

def carry_backward(carry, inputs):
    running, next_first = carry
    back_blk, first_doc, last_doc = inputs
    returning = jnp.where(next_first == last_doc, running, 0.0)
    running = back_blk + jnp.where(next_first == first_doc, running, 0.0)
    return ((running, first_doc), returning)

def reference(query_vec, key_vec, value_vec, cotangent, norm_gain, doc_ids, lang_ids, loss_table):
    block_count = TOKENS // TOK_DEV
    norm_width = HEADS * HEAD_DIM

    def split_blocks(tensor):
        return tensor.reshape(block_count, TOK_DEV, HEADS, HEAD_DIM)
    queries = split_blocks(query_vec)
    keys_all = split_blocks(key_vec)
    values_all = split_blocks(value_vec)
    doc_blocks = doc_ids.reshape(block_count, TOK_DEV)
    first_docs = doc_blocks[:, 0]
    last_docs = doc_blocks[:, TOK_DEV - 1]
    states = lax.map(forward_state, (keys_all, values_all, doc_blocks))
    start = (jnp.zeros(states.shape[1:], jnp.float32), jnp.array(-1, jnp.int32))
    unused_carry, incoming = lax.scan(carry_forward, start, (states, first_docs, last_docs))
    incoming = rounded(incoming)
    head_out = lax.map(head_block, (queries, keys_all, values_all, doc_blocks, incoming))
    flat = head_out.reshape(TOKENS, norm_width)
    table_hit = lang_ids[:, None] == jnp.arange(NLANG, dtype=jnp.int32)[None, :]
    token_weight = lax.optimization_barrier(jnp.sum(jnp.where(table_hit, loss_table[None, :], 0.0), axis=1))
    scaled = as_float(cotangent) * token_weight[:, None]
    upstream = scaled * norm_gain[None, :]
    inv_rms = lax.rsqrt(lax.optimization_barrier(jnp.sum(flat * flat, axis=1)) / norm_width + EPSILON)
    mixed = lax.optimization_barrier(jnp.sum(upstream * flat, axis=1))
    grad_out = (inv_rms[:, None] * upstream - flat * (inv_rms ** 3 * mixed / norm_width)[:, None]).astype(jnp.bfloat16)
    grads = split_blocks(grad_out)
    backs = lax.map(backward_state, (queries, grads, doc_blocks))
    start_back = (jnp.zeros(backs.shape[1:], jnp.float32), jnp.array(-1, jnp.int32))
    unused_back, returning = lax.scan(carry_backward, start_back, (backs, first_docs, last_docs), reverse=True)
    returning = rounded(returning)
    grad_q, grad_k, grad_v = lax.map(grad_block, (queries, keys_all, values_all, grads, doc_blocks, incoming, returning))
    return (grad_q.reshape(TOKENS, norm_width), grad_k.reshape(TOKENS, norm_width), grad_v.reshape(TOKENS, norm_width))
```

```python
import jax
import jax.numpy as jnp
from jax import lax
from jax.sharding import PartitionSpec as P

HEAD_DIM = 128
HEADS = 16


EPSILON = 1e-06


def shift(payload, step):
    count = lax.axis_size("seq")
    pairs = [(i, i + step) for i in range(count) if 0 <= i + step < count]
    return lax.ppermute(payload, "seq", pairs)


def pack(state, doc):
    return jnp.concatenate([state, jnp.full((8, HEAD_DIM), doc + 1.0, jnp.float32)])


def taken(payload, doc):
    return jnp.where(payload[-1, 0] == doc + 1.0, payload[:-8], 0.0)


def carried_state(own_state, own_doc, target_doc, step):
    shape = own_state.shape
    own = own_state.reshape(-1, HEAD_DIM)
    pair = pack(own + taken(shift(pack(own, own_doc), step), own_doc), own_doc)
    near, far = shift(pair, step), shift(pair, 3 * step)
    return (taken(near, target_doc) + taken(far, target_doc)).reshape(shape)


def head_sum(rows):
    count = lax.axis_size("head")
    copies = jnp.broadcast_to(rows[None], (count,) + rows.shape)
    return jnp.sum(lax.all_to_all(copies, "head", 0, 0), axis=0)


def local(query_vec, key_vec, value_vec, cotangent, norm_gain, doc_ids, lang_ids, loss_table):
    row_count = query_vec.shape[0]
    col_count = query_vec.shape[1]
    head_count = col_count // HEAD_DIM
    norm_width = HEADS * HEAD_DIM

    def split_heads(tensor):
        return tensor.reshape(row_count, head_count, HEAD_DIM)

    queries = split_heads(query_vec)
    keys_here = split_heads(key_vec)
    values_here = split_heads(value_vec)
    position = jnp.arange(row_count)
    visible = (position[:, None] >= position[None, :]) & (doc_ids[:, None] == doc_ids[None, :])
    first_doc = doc_ids[0]
    last_doc = doc_ids[row_count - 1]
    in_first = (doc_ids == first_doc)[:, None, None]
    in_last = (doc_ids == last_doc)[:, None, None]
    first_float = first_doc.astype(jnp.float32)
    last_float = last_doc.astype(jnp.float32)
    zero_bf = jnp.zeros((), jnp.bfloat16)
    kept_keys = jnp.where(in_last, keys_here, zero_bf)
    own_state = jnp.einsum(
        "the,thf->hef", kept_keys, values_here, preferred_element_type=jnp.float32
    )
    incoming = carried_state(own_state, last_float, first_float, 1).astype(jnp.bfloat16)
    raw_scores = jnp.einsum("the,she->hts", queries, keys_here, preferred_element_type=jnp.float32)
    scores = jnp.where(visible[None], raw_scores, 0.0).astype(jnp.bfloat16)
    inner = jnp.einsum("hts,shf->thf", scores, values_here, preferred_element_type=jnp.float32)
    carried = jnp.einsum("the,hef->thf", queries, incoming, preferred_element_type=jnp.float32)
    head_out = (inner + jnp.where(in_first, carried, 0.0)).reshape(row_count, col_count)
    table_hit = lang_ids[:, None] == jnp.arange(loss_table.shape[0], dtype=jnp.int32)[None, :]
    token_weight = jnp.sum(jnp.where(table_hit, loss_table[None, :], 0.0), axis=1)
    upstream = cotangent.astype(jnp.float32) * token_weight[:, None] * norm_gain[None, :]
    squares = jnp.sum(head_out * head_out, axis=1)
    mixed = jnp.sum(upstream * head_out, axis=1)
    sums = head_sum(jnp.concatenate([squares, mixed]).reshape(-1, 128)).reshape(2, row_count)
    squares, mixed = sums[0], sums[1]
    inv_rms = lax.rsqrt(squares / norm_width + EPSILON)
    grad_out = (
        inv_rms[:, None] * upstream - head_out * (inv_rms**3 * mixed / norm_width)[:, None]
    ).astype(jnp.bfloat16)
    grads = split_heads(grad_out)
    kept_queries = jnp.where(in_first, queries, zero_bf)
    own_back = jnp.einsum("the,thf->hef", kept_queries, grads, preferred_element_type=jnp.float32)
    returning = carried_state(own_back, first_float, last_float, -1).astype(jnp.bfloat16)
    grad_raw = jnp.einsum("thf,shf->hts", grads, values_here, preferred_element_type=jnp.float32)
    grad_scores = jnp.where(visible[None], grad_raw, 0.0).astype(jnp.bfloat16)
    grad_q = jnp.einsum("hts,she->the", grad_scores, keys_here, preferred_element_type=jnp.float32)
    grad_q = grad_q + jnp.where(
        in_first,
        jnp.einsum("thf,hef->the", grads, incoming, preferred_element_type=jnp.float32),
        0.0,
    )
    grad_k = jnp.einsum("hts,the->she", grad_scores, queries, preferred_element_type=jnp.float32)
    grad_k = grad_k + jnp.where(
        in_last,
        jnp.einsum("shf,hef->she", values_here, returning, preferred_element_type=jnp.float32),
        0.0,
    )
    grad_v = jnp.einsum("hts,thf->shf", scores, grads, preferred_element_type=jnp.float32)
    grad_v = grad_v + jnp.where(
        in_last,
        jnp.einsum("she,hef->shf", keys_here, returning, preferred_element_type=jnp.float32),
        0.0,
    )
    return (
        grad_q.reshape(row_count, col_count).astype(jnp.bfloat16),
        grad_k.reshape(row_count, col_count).astype(jnp.bfloat16),
        grad_v.reshape(row_count, col_count).astype(jnp.bfloat16),
    )


def solution(mesh):
    in_specs = (
        P("seq", "head"),
        P("seq", "head"),
        P("seq", "head"),
        P("seq", "head"),
        P("head"),
        P("seq"),
        P("seq"),
        P(),
    )
    out_specs = (P("seq", "head"), P("seq", "head"), P("seq", "head"))
    return jax.shard_map(local, mesh=mesh, in_specs=in_specs, out_specs=out_specs, check_vma=False)
```

```python
import jax
import jax.numpy as jnp
from jax import lax
from jax.experimental import pallas as pl
from jax.experimental.pallas import tpu as pltpu
from jax.sharding import PartitionSpec as P

HEAD_DIM = 128
HEADS = 16
NORM_WIDTH = HEADS * HEAD_DIM
EPSILON = 1e-06
TILE = 256
LANES = 128

F32 = jnp.float32
BF16 = jnp.bfloat16


def dot_nt(a, b):
    return lax.dot_general(a, b, (((1,), (1,)), ((), ())), preferred_element_type=F32)


def dot_nn(a, b):
    return lax.dot_general(a, b, (((1,), (0,)), ((), ())), preferred_element_type=F32)


def dot_tn(a, b):
    return lax.dot_general(a, b, (((0,), (0,)), ((), ())), preferred_element_type=F32)


def head_of(h):
    return slice(h * HEAD_DIM, (h + 1) * HEAD_DIM)


def down(rows):
    return jnp.concatenate(
        [
            jnp.broadcast_to(rows[i : i + 1, :], (LANES, LANES)).T
            for i in range(rows.shape[0])
        ]
    )


def across(rows):
    return jnp.concatenate([rows[i : i + 1, :] for i in range(rows.shape[0])], axis=1)


def lifted(columns):
    eye = lax.broadcasted_iota(jnp.int32, (LANES, LANES), 0) == lax.broadcasted_iota(
        jnp.int32, (LANES, LANES), 1
    )
    count = columns.shape[0] // LANES
    return jnp.concatenate(
        [
            jnp.sum(
                jnp.where(eye, columns[i * LANES : (i + 1) * LANES, :], 0.0), axis=0, keepdims=True
            )
            for i in range(count)
        ]
    )


def floats(doc_ref):
    return doc_ref[...].astype(F32)


def first_of(rows):
    return rows[0:1, 0:1]


def last_of(rows):
    return rows[-1:, LANES - 1 : LANES]


def wide(column):
    return jnp.concatenate([column, column], axis=1)


def masked_scores(left, right, doc_left, doc_right, lower):
    raw = dot_nt(left, right)
    keep = wide(doc_left) == doc_right[:, :TILE]
    width = right.shape[0]
    parts = []
    row = lax.broadcasted_iota(jnp.int32, (TILE, TILE), 0)
    col = lax.broadcasted_iota(jnp.int32, (TILE, TILE), 1)
    on_diagonal = (col <= row) if lower else (row <= col)
    for start in range(0, width, TILE):
        keep = wide(doc_left) == doc_right[:, start : start + TILE]
        if start == (width - TILE if lower else 0):
            keep = keep & on_diagonal
        parts.append(jnp.where(keep, raw[:, start : start + TILE], 0.0).astype(BF16))
    return jnp.concatenate(parts, axis=1) if len(parts) > 1 else parts[0]


def state_kernel(last, left_ref, right_ref, doc_ref, out_ref):
    rows = floats(doc_ref)
    doc = last_of(rows) if last else first_of(rows)
    keep = down(rows) == doc
    for h in range(2):
        kept = jnp.where(keep, left_ref[:, head_of(h)].astype(F32), 0.0).astype(BF16)
        out_ref[head_of(h), :] = dot_tn(kept, right_ref[:, head_of(h)])
    out_ref[256:264, :] = jnp.broadcast_to(doc + 1.0, (8, LANES))


def pair_kernel(own_ref, got_ref, out_ref):
    same = own_ref[256:257, :] == got_ref[256:257, :]
    out_ref[0:256, :] = own_ref[0:256, :] + jnp.where(same, got_ref[0:256, :], 0.0)
    out_ref[256:264, :] = own_ref[256:264, :]


def window_sum(near_ref, far_ref, doc):
    mark = doc + 1.0
    near = jnp.where(near_ref[256:257, :] == mark, near_ref[0:256, :], 0.0)
    far = jnp.where(far_ref[256:257, :] == mark, far_ref[0:256, :], 0.0)
    return (near + far).astype(BF16)


def inner_kernel(
    query_ref, key_ref, value_ref, cot_ref, gain_ref, doc_ref, lang_ref, table_ref,
    inner_ref, up_ref,
):
    rows = floats(doc_ref)
    doc_down, doc_across = down(rows), across(rows)
    lang = lang_ref[...]
    weight = jnp.zeros(lang.shape, F32)
    for n in range(table_ref.shape[1]):
        weight = weight + jnp.where(lang == n, table_ref[0:1, n : n + 1], 0.0)
    up_ref[...] = cot_ref[...].astype(F32) * wide(down(weight)) * gain_ref[...]
    count = query_ref.shape[0]
    for top in range(0, count, TILE):
        here, upto = slice(top, top + TILE), slice(0, top + TILE)
        for h in range(2):
            scores = masked_scores(
                query_ref[here, head_of(h)], key_ref[upto, head_of(h)],
                doc_down[here], doc_across[:, upto], True,
            )
            inner_ref[here, head_of(h)] = dot_nn(scores, value_ref[upto, head_of(h)])


def out_kernel(
    query_ref, inner_ref, up_ref, near_ref, far_ref, doc_ref, out_ref, incoming_ref, sums_ref
):
    rows = floats(doc_ref)
    first = first_of(rows)
    incoming = window_sum(near_ref, far_ref, first)
    incoming_ref[...] = incoming
    keep = down(rows) == first
    squares = mixed = 0.0
    for h in range(2):
        carried = dot_nn(query_ref[:, head_of(h)], incoming[head_of(h)])
        head_out = inner_ref[:, head_of(h)] + jnp.where(keep, carried, 0.0)
        out_ref[:, head_of(h)] = head_out
        squares = squares + head_out * head_out
        mixed = mixed + head_out * up_ref[:, head_of(h)]
    sums = jnp.concatenate(
        [
            lifted(jnp.sum(squares, axis=1, keepdims=True)),
            lifted(jnp.sum(mixed, axis=1, keepdims=True)),
        ]
    )
    for i in range(sums_ref.shape[0]):
        sums_ref[i] = sums


def grad_kernel(sums_ref, out_ref, up_ref, query_ref, doc_ref, grad_ref, state_ref):
    sums = sums_ref[0]
    for i in range(1, sums_ref.shape[0]):
        sums = sums + sums_ref[i]
    half = sums.shape[0] // 2
    inv = lax.rsqrt(sums[:half] / NORM_WIDTH + EPSILON)
    inv_down = down(inv)
    coef_down = down(inv * inv * inv * sums[half:] / NORM_WIDTH)
    rows = floats(doc_ref)
    first = first_of(rows)
    keep = down(rows) == first
    for h in range(2):
        grad = (inv_down * up_ref[:, head_of(h)] - out_ref[:, head_of(h)] * coef_down).astype(BF16)
        grad_ref[:, head_of(h)] = grad
        kept = jnp.where(keep, query_ref[:, head_of(h)].astype(F32), 0.0).astype(BF16)
        state_ref[head_of(h), :] = dot_tn(kept, grad)
    state_ref[256:264, :] = jnp.broadcast_to(first + 1.0, (8, LANES))


def query_kernel(key_ref, value_ref, grad_ref, incoming_ref, doc_ref, out_ref):
    rows = floats(doc_ref)
    first = first_of(rows)
    doc_down, doc_across = down(rows), across(rows)
    count = key_ref.shape[0]
    for top in range(0, count, TILE):
        here, upto = slice(top, top + TILE), slice(0, top + TILE)
        for h in range(2):
            grad = grad_ref[here, head_of(h)]
            scores = masked_scores(
                grad, value_ref[upto, head_of(h)], doc_down[here], doc_across[:, upto], True
            )
            carried = dot_nt(grad, incoming_ref[head_of(h), :])
            total = dot_nn(scores, key_ref[upto, head_of(h)])
            total = total + jnp.where(doc_down[here] == first, carried, 0.0)
            out_ref[here, head_of(h)] = total.astype(BF16)


def key_value_kernel(query_ref, key_ref, value_ref, grad_ref, doc_ref, gkey_ref, gvalue_ref):
    rows = floats(doc_ref)
    doc_down, doc_across = down(rows), across(rows)
    count = key_ref.shape[0]
    for top in range(0, count, TILE):
        here, rest = slice(top, top + TILE), slice(top, count)
        for h in range(2):
            query, grad = query_ref[rest, head_of(h)], grad_ref[rest, head_of(h)]
            docs = (doc_down[here], doc_across[:, rest])
            back = masked_scores(value_ref[here, head_of(h)], grad, *docs, False)
            gkey_ref[here, head_of(h)] = dot_nn(back, query)
            scores = masked_scores(key_ref[here, head_of(h)], query, *docs, False)
            gvalue_ref[here, head_of(h)] = dot_nn(scores, grad)


def last_kernel(
    key_ref, value_ref, gkey_ref, gvalue_ref, near_ref, far_ref, doc_ref, okey_ref, ovalue_ref
):
    rows = floats(doc_ref)
    last = last_of(rows)
    keep = down(rows) == last
    returning = window_sum(near_ref, far_ref, last)
    for h in range(2):
        state = returning[head_of(h)]
        key = dot_nt(value_ref[:, head_of(h)], state)
        okey_ref[:, head_of(h)] = (gkey_ref[:, head_of(h)] + jnp.where(keep, key, 0.0)).astype(BF16)
        value = dot_nn(key_ref[:, head_of(h)], state)
        ovalue_ref[:, head_of(h)] = (
            gvalue_ref[:, head_of(h)] + jnp.where(keep, value, 0.0)
        ).astype(BF16)


def run(kernel, outs, args, flops=0, name=None):
    shapes = tuple(jax.ShapeDtypeStruct(shape, dtype) for shape, dtype in outs)
    moved = sum(a.size * a.dtype.itemsize for a in (*args, *shapes))
    whole = pl.BlockSpec(memory_space=pltpu.VMEM)
    got = pl.pallas_call(
        kernel,
        out_shape=shapes,
        in_specs=[whole] * len(args),
        out_specs=tuple([whole] * len(shapes)),
        compiler_params=pltpu.CompilerParams(vmem_limit_bytes=32 * 1024 * 1024),
        cost_estimate=pl.CostEstimate(flops=flops, bytes_accessed=moved, transcendentals=0),
        name=name,
    )(*args)
    return got[0] if len(outs) == 1 else got


def shift(payload, step):
    count = lax.axis_size("seq")
    pairs = [(i, i + step) for i in range(count) if 0 <= i + step < count]
    return lax.ppermute(payload, "seq", pairs)


def local(query_vec, key_vec, value_vec, cotangent, norm_gain, doc_ids, lang_ids, loss_table):
    count, columns = query_vec.shape
    docs = doc_ids.reshape(-1, LANES)
    langs = lang_ids.reshape(-1, LANES)
    square = 2 * columns * count * count
    packed = ((columns + 8, LANES), F32)
    full = ((count, columns), F32)
    half = ((count, columns), BF16)

    own = run(
        lambda *refs: state_kernel(True, *refs), [packed], (key_vec, value_vec, docs), name="state"
    )
    got = shift(own, 1)
    inner, up = run(
        inner_kernel,
        [full, full],
        (
            query_vec, key_vec, value_vec, cotangent, norm_gain[None, :], docs, langs,
            loss_table[None, :],
        ),
        flops=2 * square,
        name="inner",
    )
    pair = run(pair_kernel, [packed], (own, got), name="pair")
    near, far = shift(pair, 1), shift(pair, 3)
    heads = lax.axis_size("head")
    head_out, incoming, sums = run(
        out_kernel,
        [full, ((columns, LANES), BF16), ((heads, 2 * count // LANES, LANES), F32)],
        (query_vec, inner, up, near, far, docs),
        name="out",
    )
    sums = lax.all_to_all(sums, "head", 0, 0)
    grad, own_back = run(
        grad_kernel, [half, packed], (sums, head_out, up, query_vec, docs), name="grad"
    )
    got_back = shift(own_back, -1)
    grad_q = run(
        query_kernel,
        [half],
        (key_vec, value_vec, grad, incoming, docs),
        flops=2 * square,
        name="query",
    )
    pair_back = run(pair_kernel, [packed], (own_back, got_back), name="pair_back")
    near_back, far_back = shift(pair_back, -1), shift(pair_back, -3)
    part_k, part_v = run(
        key_value_kernel,
        [full, full],
        (query_vec, key_vec, value_vec, grad, docs),
        flops=4 * square,
        name="key_value",
    )
    grad_k, grad_v = run(
        last_kernel,
        [half, half],
        (key_vec, value_vec, part_k, part_v, near_back, far_back, docs),
        name="last",
    )
    return grad_q, grad_k, grad_v


def solution(mesh):
    in_specs = (
        P("seq", "head"),
        P("seq", "head"),
        P("seq", "head"),
        P("seq", "head"),
        P("head"),
        P("seq"),
        P("seq"),
        P(),
    )
    out_specs = (P("seq", "head"), P("seq", "head"), P("seq", "head"))
    return jax.shard_map(local, mesh=mesh, in_specs=in_specs, out_specs=out_specs, check_vma=False)
```

```python
import jax
import jax.numpy as jnp
from jax import lax
from jax.experimental import pallas as pl
from jax.experimental.pallas import tpu as pltpu
from jax.sharding import PartitionSpec as P

HEAD_DIM = 128
HEADS = 16
NORM_WIDTH = HEADS * HEAD_DIM
EPSILON = 1e-06
TILE = 256
LANES = 128

F32 = jnp.float32
BF16 = jnp.bfloat16


def dot_nt(a, b):
    return lax.dot_general(a, b, (((1,), (1,)), ((), ())), preferred_element_type=F32)


def dot_nn(a, b):
    return lax.dot_general(a, b, (((1,), (0,)), ((), ())), preferred_element_type=F32)


def dot_tn(a, b):
    return lax.dot_general(a, b, (((0,), (0,)), ((), ())), preferred_element_type=F32)


def head_of(h):
    return slice(h * HEAD_DIM, (h + 1) * HEAD_DIM)


def down(rows):
    return jnp.concatenate(
        [
            jnp.broadcast_to(rows[i : i + 1, :], (LANES, LANES)).T
            for i in range(rows.shape[0])
        ]
    )


def across(rows):
    return jnp.concatenate([rows[i : i + 1, :] for i in range(rows.shape[0])], axis=1)


def lifted(columns):
    eye = lax.broadcasted_iota(jnp.int32, (LANES, LANES), 0) == lax.broadcasted_iota(
        jnp.int32, (LANES, LANES), 1
    )
    count = columns.shape[0] // LANES
    return jnp.concatenate(
        [
            jnp.sum(
                jnp.where(eye, columns[i * LANES : (i + 1) * LANES, :], 0.0), axis=0, keepdims=True
            )
            for i in range(count)
        ]
    )


def floats(doc_ref):
    return doc_ref[...].astype(F32)


def first_of(rows):
    return rows[0:1, 0:1]


def last_of(rows):
    return rows[-1:, LANES - 1 : LANES]


def wide(column):
    return jnp.concatenate([column, column], axis=1)


def masked_scores(left, right, doc_left, doc_right, lower):
    raw = dot_nt(left, right)
    width = right.shape[0]
    parts = []
    row = lax.broadcasted_iota(jnp.int32, (TILE, TILE), 0)
    col = lax.broadcasted_iota(jnp.int32, (TILE, TILE), 1)
    on_diagonal = (col <= row) if lower else (row <= col)
    for start in range(0, width, TILE):
        keep = wide(doc_left) == doc_right[:, start : start + TILE]
        if start == (width - TILE if lower else 0):
            keep = keep & on_diagonal
        parts.append(jnp.where(keep, raw[:, start : start + TILE], 0.0).astype(BF16))
    return jnp.concatenate(parts, axis=1) if len(parts) > 1 else parts[0]


def state_kernel(key_hbm, value_hbm, doc_hbm, out_ref, key_ref, value_ref, doc_ref, sems):
    count = key_ref.shape[0]
    halves = [slice(0, count // 2), slice(count // 2, count)]
    copies = [pltpu.make_async_copy(doc_hbm, doc_ref, sems.at[0])]
    for i, part in enumerate(halves):
        copies.append(pltpu.make_async_copy(key_hbm.at[part], key_ref.at[part], sems.at[1 + 2 * i]))
        copies.append(
            pltpu.make_async_copy(value_hbm.at[part], value_ref.at[part], sems.at[2 + 2 * i])
        )
    for copy in copies:
        copy.start()
    copies[0].wait()
    rows = floats(doc_ref)
    doc = last_of(rows)
    keep = down(rows) == doc
    totals = [0.0, 0.0]
    for i, part in enumerate(halves):
        copies[1 + 2 * i].wait()
        copies[2 + 2 * i].wait()
        for h in range(2):
            kept = jnp.where(keep[part], key_ref[part, head_of(h)].astype(F32), 0.0).astype(BF16)
            totals[h] = totals[h] + dot_tn(kept, value_ref[part, head_of(h)])
    for h in range(2):
        out_ref[head_of(h), :] = totals[h]
    out_ref[256:264, :] = jnp.broadcast_to(doc + 1.0, (8, LANES))


def pair_kernel(own_ref, got_ref, out_ref):
    same = own_ref[256:257, :] == got_ref[256:257, :]
    out_ref[0:256, :] = own_ref[0:256, :] + jnp.where(same, got_ref[0:256, :], 0.0)
    out_ref[256:264, :] = own_ref[256:264, :]


def window_sum(near_ref, far_ref, doc):
    mark = doc + 1.0
    near = jnp.where(near_ref[256:257, :] == mark, near_ref[0:256, :], 0.0)
    far = jnp.where(far_ref[256:257, :] == mark, far_ref[0:256, :], 0.0)
    return (near + far).astype(BF16)


def inner_kernel(
    query_ref, key_ref, value_ref, doc_ref, cot_hbm, gain_hbm, lang_hbm, table_hbm,
    inner_ref, up_ref, cot_ref, gain_ref, lang_ref, table_ref, sems,
):
    pairs = ((cot_hbm, cot_ref), (gain_hbm, gain_ref), (lang_hbm, lang_ref), (table_hbm, table_ref))
    copies = [
        pltpu.make_async_copy(hbm, ref, sems.at[i]) for i, (hbm, ref) in enumerate(pairs)
    ]
    for copy in copies:
        copy.start()
    rows = floats(doc_ref)
    doc_down, doc_across = down(rows), across(rows)
    count = query_ref.shape[0]
    for top in range(0, count, TILE):
        here, upto = slice(top, top + TILE), slice(0, top + TILE)
        for h in range(2):
            scores = masked_scores(
                query_ref[here, head_of(h)], key_ref[upto, head_of(h)],
                doc_down[here], doc_across[:, upto], True,
            )
            inner_ref[here, head_of(h)] = dot_nn(scores, value_ref[upto, head_of(h)])
    for copy in copies:
        copy.wait()
    lang = lang_ref[...]
    weight = jnp.zeros(lang.shape, F32)
    for n in range(table_ref.shape[1]):
        weight = weight + jnp.where(lang == n, table_ref[0:1, n : n + 1], 0.0)
    up_ref[...] = cot_ref[...].astype(F32) * wide(down(weight)) * gain_ref[...]


def out_kernel(
    query_ref, inner_ref, up_ref, near_ref, far_ref, doc_ref, out_ref, incoming_ref, sums_ref
):
    rows = floats(doc_ref)
    first = first_of(rows)
    incoming = window_sum(near_ref, far_ref, first)
    incoming_ref[...] = incoming
    keep = down(rows) == first
    squares = mixed = 0.0
    for h in range(2):
        carried = dot_nn(query_ref[:, head_of(h)], incoming[head_of(h)])
        head_out = inner_ref[:, head_of(h)] + jnp.where(keep, carried, 0.0)
        out_ref[:, head_of(h)] = head_out
        squares = squares + head_out * head_out
        mixed = mixed + head_out * up_ref[:, head_of(h)]
    sums = jnp.concatenate(
        [
            lifted(jnp.sum(squares, axis=1, keepdims=True)),
            lifted(jnp.sum(mixed, axis=1, keepdims=True)),
        ]
    )
    for i in range(sums_ref.shape[0]):
        sums_ref[i] = sums


def grad_kernel(sums_ref, out_ref, up_ref, query_ref, doc_ref, grad_ref, state_ref):
    sums = sums_ref[0]
    for i in range(1, sums_ref.shape[0]):
        sums = sums + sums_ref[i]
    half = sums.shape[0] // 2
    inv = lax.rsqrt(sums[:half] / NORM_WIDTH + EPSILON)
    inv_down = down(inv)
    coef_down = down(inv * inv * inv * sums[half:] / NORM_WIDTH)
    rows = floats(doc_ref)
    first = first_of(rows)
    keep = down(rows) == first
    for h in range(2):
        grad = (inv_down * up_ref[:, head_of(h)] - out_ref[:, head_of(h)] * coef_down).astype(BF16)
        grad_ref[:, head_of(h)] = grad
        kept = jnp.where(keep, query_ref[:, head_of(h)].astype(F32), 0.0).astype(BF16)
        state_ref[head_of(h), :] = dot_tn(kept, grad)
    state_ref[256:264, :] = jnp.broadcast_to(first + 1.0, (8, LANES))


def query_kernel(key_ref, value_ref, grad_ref, incoming_ref, doc_ref, out_ref):
    rows = floats(doc_ref)
    first = first_of(rows)
    doc_down, doc_across = down(rows), across(rows)
    count = key_ref.shape[0]
    for top in range(0, count, TILE):
        here, upto = slice(top, top + TILE), slice(0, top + TILE)
        for h in range(2):
            grad = grad_ref[here, head_of(h)]
            scores = masked_scores(
                grad, value_ref[upto, head_of(h)], doc_down[here], doc_across[:, upto], True
            )
            carried = dot_nt(grad, incoming_ref[head_of(h), :])
            total = dot_nn(scores, key_ref[upto, head_of(h)])
            total = total + jnp.where(doc_down[here] == first, carried, 0.0)
            out_ref[here, head_of(h)] = total.astype(BF16)


def key_value_kernel(
    query_ref, key_ref, value_ref, grad_ref, doc_ref, gquery_ref, gkey_ref, gvalue_ref, out_hbm, sem
):
    copy = pltpu.make_async_copy(gquery_ref, out_hbm, sem)
    copy.start()
    rows = floats(doc_ref)
    doc_down, doc_across = down(rows), across(rows)
    count = key_ref.shape[0]
    for top in range(0, count, TILE):
        here, rest = slice(top, top + TILE), slice(top, count)
        for h in range(2):
            query, grad = query_ref[rest, head_of(h)], grad_ref[rest, head_of(h)]
            docs = (doc_down[here], doc_across[:, rest])
            back = masked_scores(value_ref[here, head_of(h)], grad, *docs, False)
            gkey_ref[here, head_of(h)] = dot_nn(back, query)
            scores = masked_scores(key_ref[here, head_of(h)], query, *docs, False)
            gvalue_ref[here, head_of(h)] = dot_nn(scores, grad)
    copy.wait()


def last_kernel(
    key_ref, value_ref, gkey_ref, gvalue_ref, near_ref, far_ref, doc_ref,
    okey_hbm, ovalue_hbm, okey_ref, ovalue_ref, sems,
):
    rows = floats(doc_ref)
    last = last_of(rows)
    keep = down(rows) == last
    returning = window_sum(near_ref, far_ref, last)
    copies = []
    for top in range(0, key_ref.shape[0], TILE):
        here = slice(top, top + TILE)
        for h in range(2):
            state = returning[head_of(h)]
            key = dot_nt(value_ref[here, head_of(h)], state)
            key = gkey_ref[here, head_of(h)] + jnp.where(keep[here], key, 0.0)
            okey_ref[here, head_of(h)] = key.astype(BF16)
            value = dot_nn(key_ref[here, head_of(h)], state)
            value = gvalue_ref[here, head_of(h)] + jnp.where(keep[here], value, 0.0)
            ovalue_ref[here, head_of(h)] = value.astype(BF16)
        for ref, hbm in ((okey_ref, okey_hbm), (ovalue_ref, ovalue_hbm)):
            copies.append(pltpu.make_async_copy(ref.at[here], hbm.at[here], sems.at[len(copies)]))
            copies[-1].start()
    for copy in copies:
        copy.wait()


def run(kernel, outs, args, flops=0, name=None, far_ins=(), far_outs=(), scratch=(), limit=32):
    shapes = tuple(jax.ShapeDtypeStruct(shape, dtype) for shape, dtype in outs)
    moved = sum(a.size * a.dtype.itemsize for a in (*args, *shapes))
    near, far = pl.BlockSpec(memory_space=pltpu.VMEM), pl.BlockSpec(memory_space=pltpu.HBM)
    got = pl.pallas_call(
        kernel,
        out_shape=shapes,
        in_specs=[far if i in far_ins else near for i in range(len(args))],
        out_specs=tuple(far if i in far_outs else near for i in range(len(shapes))),
        scratch_shapes=scratch,
        compiler_params=pltpu.CompilerParams(vmem_limit_bytes=limit * 1024 * 1024),
        cost_estimate=pl.CostEstimate(flops=flops, bytes_accessed=moved, transcendentals=0),
        name=name,
    )(
        *(
            pltpu.with_memory_space_constraint(a, pltpu.HBM) if i in far_ins else a
            for i, a in enumerate(args)
        )
    )
    return got[0] if len(outs) == 1 else got


def shift(payload, step):
    count = lax.axis_size("seq")
    pairs = [(i, i + step) for i in range(count) if 0 <= i + step < count]
    return lax.ppermute(payload, "seq", pairs)


def local(query_vec, key_vec, value_vec, cotangent, norm_gain, doc_ids, lang_ids, loss_table):
    count, columns = query_vec.shape
    docs = doc_ids.reshape(-1, LANES)
    langs = lang_ids.reshape(-1, LANES)
    square = 2 * columns * count * count
    packed = ((columns + 8, LANES), F32)
    full = ((count, columns), F32)
    half = ((count, columns), BF16)

    own = run(
        state_kernel,
        [packed],
        (key_vec, value_vec, docs),
        name="state",
        far_ins=(0, 1, 2),
        scratch=[
            pltpu.VMEM((count, columns), BF16),
            pltpu.VMEM((count, columns), BF16),
            pltpu.VMEM(docs.shape, jnp.int32),
            pltpu.SemaphoreType.DMA((5,)),
        ],
    )
    got = shift(own, 1)
    inner, up = run(
        inner_kernel,
        [full, full],
        (
            query_vec, key_vec, value_vec, docs, cotangent, norm_gain[None, :], langs,
            loss_table[None, :],
        ),
        flops=2 * square,
        name="inner",
        far_ins=(4, 5, 6, 7),
        scratch=[
            pltpu.VMEM((count, columns), BF16),
            pltpu.VMEM((1, columns), F32),
            pltpu.VMEM(langs.shape, jnp.int32),
            pltpu.VMEM((1, loss_table.shape[0]), F32),
            pltpu.SemaphoreType.DMA((4,)),
        ],
    )
    pair = run(pair_kernel, [packed], (own, got), name="pair")
    near, far = shift(pair, 1), shift(pair, 3)
    heads = lax.axis_size("head")
    head_out, incoming, sums = run(
        out_kernel,
        [full, ((columns, LANES), BF16), ((heads, 2 * count // LANES, LANES), F32)],
        (query_vec, inner, up, near, far, docs),
        name="out",
    )
    sums = lax.all_to_all(sums, "head", 0, 0)
    grad, own_back = run(
        grad_kernel, [half, packed], (sums, head_out, up, query_vec, docs), name="grad"
    )
    got_back = shift(own_back, -1)
    part_q = run(
        query_kernel,
        [half],
        (key_vec, value_vec, grad, incoming, docs),
        flops=2 * square,
        name="query",
    )
    pair_back = run(
        lambda own_ref, got_ref, _, out_ref: pair_kernel(own_ref, got_ref, out_ref),
        [packed],
        (own_back, got_back, part_q),
        name="pair_back",
    )
    near_back, far_back = shift(pair_back, -1), shift(pair_back, -3)
    part_k, part_v, grad_q = run(
        key_value_kernel,
        [full, full, half],
        (query_vec, key_vec, value_vec, grad, docs, part_q),
        flops=4 * square,
        name="key_value",
        far_outs=(2,),
        scratch=[pltpu.SemaphoreType.DMA],
    )
    grad_k, grad_v = run(
        last_kernel,
        [half, half],
        (key_vec, value_vec, part_k, part_v, near_back, far_back, docs),
        name="last",
        far_outs=(0, 1),
        scratch=[
            pltpu.VMEM((count, columns), BF16),
            pltpu.VMEM((count, columns), BF16),
            pltpu.SemaphoreType.DMA((2 * count // TILE,)),
        ],
    )
    return grad_q, grad_k, grad_v


def solution(mesh):
    in_specs = (
        P("seq", "head"),
        P("seq", "head"),
        P("seq", "head"),
        P("seq", "head"),
        P("head"),
        P("seq"),
        P("seq"),
        P(),
    )
    out_specs = (P("seq", "head"), P("seq", "head"), P("seq", "head"))
    return jax.shard_map(local, mesh=mesh, in_specs=in_specs, out_specs=out_specs, check_vma=False)
```

```python
import jax
import jax.numpy as jnp
from jax import lax
from jax.experimental import pallas as pl
from jax.experimental.pallas import tpu as pltpu
from jax.sharding import PartitionSpec as P

HEAD_DIM = 128
HEADS = 16
NORM_WIDTH = HEADS * HEAD_DIM
EPSILON = 1e-06
TILE = 256
LANES = 128

F32 = jnp.float32
BF16 = jnp.bfloat16


def dot_nt(a, b):
    return lax.dot_general(a, b, (((1,), (1,)), ((), ())), preferred_element_type=F32)


def dot_nn(a, b):
    return lax.dot_general(a, b, (((1,), (0,)), ((), ())), preferred_element_type=F32)


def dot_tn(a, b):
    return lax.dot_general(a, b, (((0,), (0,)), ((), ())), preferred_element_type=F32)


def head_of(h):
    return slice(h * HEAD_DIM, (h + 1) * HEAD_DIM)


def down(rows):
    return jnp.concatenate(
        [
            jnp.broadcast_to(rows[i : i + 1, :], (LANES, LANES)).T
            for i in range(rows.shape[0])
        ]
    )


def across(rows):
    return jnp.concatenate([rows[i : i + 1, :] for i in range(rows.shape[0])], axis=1)


def lifted(columns):
    eye = lax.broadcasted_iota(jnp.int32, (LANES, LANES), 0) == lax.broadcasted_iota(
        jnp.int32, (LANES, LANES), 1
    )
    count = columns.shape[0] // LANES
    return jnp.concatenate(
        [
            jnp.sum(
                jnp.where(eye, columns[i * LANES : (i + 1) * LANES, :], 0.0), axis=0, keepdims=True
            )
            for i in range(count)
        ]
    )


def floats(doc_ref):
    return doc_ref[...].astype(F32)


def first_of(rows):
    return rows[0:1, 0:1]


def last_of(rows):
    return rows[-1:, LANES - 1 : LANES]


def tokens_of(rows, doc):
    hit = jnp.where(rows == doc, 1.0, 0.0)
    return jnp.sum(jnp.sum(hit, axis=0, keepdims=True), axis=1, keepdims=True)


def token_numbers(rows):
    return lax.broadcasted_iota(jnp.int32, (rows.size, LANES), 0).astype(F32)


def in_first(rows):
    return token_numbers(rows) < tokens_of(rows, first_of(rows))


def in_last(rows):
    return token_numbers(rows) >= rows.size - tokens_of(rows, last_of(rows))


def wide(column):
    return jnp.concatenate([column, column], axis=1)


def masked_scores(left, right, doc_left, doc_right, lower):
    raw = dot_nt(left, right)
    width = right.shape[0]
    parts = []
    row = lax.broadcasted_iota(jnp.int32, (TILE, TILE), 0)
    col = lax.broadcasted_iota(jnp.int32, (TILE, TILE), 1)
    on_diagonal = (col <= row) if lower else (row <= col)
    for start in range(0, width, TILE):
        keep = wide(doc_left) == doc_right[:, start : start + TILE]
        if start == (width - TILE if lower else 0):
            keep = keep & on_diagonal
        parts.append(jnp.where(keep, raw[:, start : start + TILE], 0.0).astype(BF16))
    return jnp.concatenate(parts, axis=1) if len(parts) > 1 else parts[0]


def state_kernel(key_hbm, value_hbm, doc_hbm, out_ref, key_ref, value_ref, doc_ref, sems):
    count = key_ref.shape[0]
    quarters = [slice(top, top + TILE) for top in range(0, count, TILE)]
    copies = [pltpu.make_async_copy(doc_hbm, doc_ref, sems.at[0])]
    for i, part in enumerate(quarters):
        copies.append(pltpu.make_async_copy(key_hbm.at[part], key_ref.at[part], sems.at[1 + 2 * i]))
        copies.append(
            pltpu.make_async_copy(value_hbm.at[part], value_ref.at[part], sems.at[2 + 2 * i])
        )
    for copy in copies:
        copy.start()
    copies[0].wait()
    rows = floats(doc_ref)
    doc = last_of(rows)
    keep = in_last(rows)
    totals = [0.0, 0.0]
    for i, part in enumerate(quarters):
        copies[1 + 2 * i].wait()
        copies[2 + 2 * i].wait()
        for h in range(2):
            kept = jnp.where(keep[part], key_ref[part, head_of(h)].astype(F32), 0.0).astype(BF16)
            totals[h] = totals[h] + dot_tn(kept, value_ref[part, head_of(h)])
    for h in range(2):
        out_ref[head_of(h), :] = totals[h]
    out_ref[256:264, :] = jnp.broadcast_to(doc + 1.0, (8, LANES))


def pair_kernel(own_ref, got_ref, out_ref):
    same = own_ref[256:257, :] == got_ref[256:257, :]
    out_ref[0:256, :] = own_ref[0:256, :] + jnp.where(same, got_ref[0:256, :], 0.0)
    out_ref[256:264, :] = own_ref[256:264, :]


def window_sum(near_ref, far_ref, doc):
    mark = doc + 1.0
    near = jnp.where(near_ref[256:257, :] == mark, near_ref[0:256, :], 0.0)
    far = jnp.where(far_ref[256:257, :] == mark, far_ref[0:256, :], 0.0)
    return (near + far).astype(BF16)


def inner_kernel(
    query_ref, key_ref, value_ref, doc_ref, cot_hbm, gain_hbm, lang_hbm, table_hbm,
    inner_ref, up_ref, cot_ref, gain_ref, lang_ref, table_ref, sems,
):
    pairs = ((cot_hbm, cot_ref), (gain_hbm, gain_ref), (lang_hbm, lang_ref), (table_hbm, table_ref))
    copies = [
        pltpu.make_async_copy(hbm, ref, sems.at[i]) for i, (hbm, ref) in enumerate(pairs)
    ]
    for copy in copies:
        copy.start()
    rows = floats(doc_ref)
    doc_down, doc_across = down(rows), across(rows)
    count = query_ref.shape[0]
    weight_down = None
    for top in range(0, count, TILE):
        here, upto = slice(top, top + TILE), slice(0, top + TILE)
        for h in range(2):
            scores = masked_scores(
                query_ref[here, head_of(h)], key_ref[upto, head_of(h)],
                doc_down[here], doc_across[:, upto], True,
            )
            inner_ref[here, head_of(h)] = dot_nn(scores, value_ref[upto, head_of(h)])
        if weight_down is None:
            for copy in copies:
                copy.wait()
            lang = lang_ref[...]
            weight = jnp.zeros(lang.shape, F32)
            for n in range(table_ref.shape[1]):
                weight = weight + jnp.where(lang == n, table_ref[0:1, n : n + 1], 0.0)
            weight_down = down(weight)
        up_ref[here] = cot_ref[here].astype(F32) * wide(weight_down[here]) * gain_ref[...]


def out_kernel(
    query_ref, inner_ref, up_ref, near_ref, far_ref, doc_ref, out_ref, incoming_ref, sums_ref
):
    rows = floats(doc_ref)
    first = first_of(rows)
    incoming = window_sum(near_ref, far_ref, first)
    incoming_ref[...] = incoming
    keep = in_first(rows)
    squares = mixed = 0.0
    for h in range(2):
        carried = dot_nn(query_ref[:, head_of(h)], incoming[head_of(h)])
        head_out = inner_ref[:, head_of(h)] + jnp.where(keep, carried, 0.0)
        out_ref[:, head_of(h)] = head_out
        squares = squares + head_out * head_out
        mixed = mixed + head_out * up_ref[:, head_of(h)]
    sums = jnp.concatenate(
        [
            lifted(jnp.sum(squares, axis=1, keepdims=True)),
            lifted(jnp.sum(mixed, axis=1, keepdims=True)),
        ]
    )
    for i in range(sums_ref.shape[0]):
        sums_ref[i] = sums


def grad_kernel(sums_ref, out_ref, up_ref, query_ref, doc_ref, grad_ref, state_ref):
    sums = sums_ref[0]
    for i in range(1, sums_ref.shape[0]):
        sums = sums + sums_ref[i]
    half = sums.shape[0] // 2
    inv = lax.rsqrt(sums[:half] / NORM_WIDTH + EPSILON)
    inv_down = down(inv)
    coef_down = down(inv * inv * inv * sums[half:] / NORM_WIDTH)
    rows = floats(doc_ref)
    first = first_of(rows)
    keep = in_first(rows)
    for h in range(2):
        grad = (inv_down * up_ref[:, head_of(h)] - out_ref[:, head_of(h)] * coef_down).astype(BF16)
        grad_ref[:, head_of(h)] = grad
        kept = jnp.where(keep, query_ref[:, head_of(h)].astype(F32), 0.0).astype(BF16)
        state_ref[head_of(h), :] = dot_tn(kept, grad)
    state_ref[256:264, :] = jnp.broadcast_to(first + 1.0, (8, LANES))


def query_kernel(key_ref, value_ref, grad_ref, incoming_ref, doc_ref, out_ref):
    rows = floats(doc_ref)
    first = first_of(rows)
    doc_down, doc_across = down(rows), across(rows)
    count = key_ref.shape[0]
    for top in range(0, count, TILE):
        here, upto = slice(top, top + TILE), slice(0, top + TILE)
        for h in range(2):
            grad = grad_ref[here, head_of(h)]
            scores = masked_scores(
                grad, value_ref[upto, head_of(h)], doc_down[here], doc_across[:, upto], True
            )
            carried = dot_nt(grad, incoming_ref[head_of(h), :])
            total = dot_nn(scores, key_ref[upto, head_of(h)])
            total = total + jnp.where(doc_down[here] == first, carried, 0.0)
            out_ref[here, head_of(h)] = total.astype(BF16)


def key_value_kernel(
    query_ref, key_ref, value_ref, grad_ref, doc_ref, gquery_ref, gkey_ref, gvalue_ref, out_hbm, sem
):
    copy = pltpu.make_async_copy(gquery_ref, out_hbm, sem)
    copy.start()
    rows = floats(doc_ref)
    doc_down, doc_across = down(rows), across(rows)
    count = key_ref.shape[0]
    for top in range(0, count, TILE):
        here, rest = slice(top, top + TILE), slice(top, count)
        for h in range(2):
            query, grad = query_ref[rest, head_of(h)], grad_ref[rest, head_of(h)]
            docs = (doc_down[here], doc_across[:, rest])
            back = masked_scores(value_ref[here, head_of(h)], grad, *docs, False)
            gkey_ref[here, head_of(h)] = dot_nn(back, query)
            scores = masked_scores(key_ref[here, head_of(h)], query, *docs, False)
            gvalue_ref[here, head_of(h)] = dot_nn(scores, grad)
    copy.wait()


def last_kernel(
    key_ref, value_ref, gkey_ref, gvalue_ref, near_ref, far_ref, doc_ref,
    okey_hbm, ovalue_hbm, okey_ref, ovalue_ref, sems,
):
    rows = floats(doc_ref)
    last = last_of(rows)
    keep = in_last(rows)
    returning = window_sum(near_ref, far_ref, last)
    copies = []
    for top in range(0, key_ref.shape[0], TILE):
        here = slice(top, top + TILE)
        for h in range(2):
            state = returning[head_of(h)]
            key = dot_nt(value_ref[here, head_of(h)], state)
            key = gkey_ref[here, head_of(h)] + jnp.where(keep[here], key, 0.0)
            okey_ref[here, head_of(h)] = key.astype(BF16)
            value = dot_nn(key_ref[here, head_of(h)], state)
            value = gvalue_ref[here, head_of(h)] + jnp.where(keep[here], value, 0.0)
            ovalue_ref[here, head_of(h)] = value.astype(BF16)
        for ref, hbm in ((okey_ref, okey_hbm), (ovalue_ref, ovalue_hbm)):
            copies.append(pltpu.make_async_copy(ref.at[here], hbm.at[here], sems.at[len(copies)]))
            copies[-1].start()
    for copy in copies:
        copy.wait()


def run(kernel, outs, args, flops=0, name=None, far_ins=(), far_outs=(), scratch=(), limit=32):
    shapes = tuple(jax.ShapeDtypeStruct(shape, dtype) for shape, dtype in outs)
    moved = sum(a.size * a.dtype.itemsize for a in (*args, *shapes))
    near, far = pl.BlockSpec(memory_space=pltpu.VMEM), pl.BlockSpec(memory_space=pltpu.HBM)
    got = pl.pallas_call(
        kernel,
        out_shape=shapes,
        in_specs=[far if i in far_ins else near for i in range(len(args))],
        out_specs=tuple(far if i in far_outs else near for i in range(len(shapes))),
        scratch_shapes=scratch,
        compiler_params=pltpu.CompilerParams(vmem_limit_bytes=limit * 1024 * 1024),
        cost_estimate=pl.CostEstimate(flops=flops, bytes_accessed=moved, transcendentals=0),
        name=name,
    )(
        *(
            pltpu.with_memory_space_constraint(a, pltpu.HBM) if i in far_ins else a
            for i, a in enumerate(args)
        )
    )
    return got[0] if len(outs) == 1 else got


def shift(payload, step):
    count = lax.axis_size("seq")
    pairs = [(i, i + step) for i in range(count) if 0 <= i + step < count]
    return lax.ppermute(payload, "seq", pairs)


def local(query_vec, key_vec, value_vec, cotangent, norm_gain, doc_ids, lang_ids, loss_table):
    count, columns = query_vec.shape
    docs = doc_ids.reshape(-1, LANES)
    langs = lang_ids.reshape(-1, LANES)
    square = 2 * columns * count * count
    packed = ((columns + 8, LANES), F32)
    full = ((count, columns), F32)
    half = ((count, columns), BF16)

    own, key_vec, value_vec = run(
        state_kernel,
        [packed, half, half],
        (key_vec, value_vec, docs),
        name="state",
        far_ins=(0, 1, 2),
        scratch=[
            pltpu.VMEM(docs.shape, jnp.int32),
            pltpu.SemaphoreType.DMA((1 + 2 * (count // TILE),)),
        ],
    )
    got = shift(own, 1)
    inner, up = run(
        inner_kernel,
        [full, full],
        (
            query_vec, key_vec, value_vec, docs, cotangent, norm_gain[None, :], langs,
            loss_table[None, :],
        ),
        flops=2 * square,
        name="inner",
        far_ins=(4, 5, 6, 7),
        scratch=[
            pltpu.VMEM((count, columns), BF16),
            pltpu.VMEM((1, columns), F32),
            pltpu.VMEM(langs.shape, jnp.int32),
            pltpu.VMEM((1, loss_table.shape[0]), F32),
            pltpu.SemaphoreType.DMA((4,)),
        ],
    )
    pair = run(pair_kernel, [packed], (own, got), name="pair")
    near, far = shift(pair, 1), shift(pair, 3)
    heads = lax.axis_size("head")
    head_out, incoming, sums = run(
        out_kernel,
        [full, ((columns, LANES), BF16), ((heads, 2 * count // LANES, LANES), F32)],
        (query_vec, inner, up, near, far, docs),
        name="out",
    )
    sums = lax.all_to_all(sums, "head", 0, 0)
    grad, own_back = run(
        grad_kernel, [half, packed], (sums, head_out, up, query_vec, docs), name="grad"
    )
    got_back = shift(own_back, -1)
    part_q = run(
        query_kernel,
        [half],
        (key_vec, value_vec, grad, incoming, docs),
        flops=2 * square,
        name="query",
    )
    pair_back = run(
        lambda own_ref, got_ref, _, out_ref: pair_kernel(own_ref, got_ref, out_ref),
        [packed],
        (own_back, got_back, part_q),
        name="pair_back",
    )
    near_back, far_back = shift(pair_back, -1), shift(pair_back, -3)
    part_k, part_v, grad_q = run(
        key_value_kernel,
        [full, full, half],
        (query_vec, key_vec, value_vec, grad, docs, part_q),
        flops=4 * square,
        name="key_value",
        far_outs=(2,),
        scratch=[pltpu.SemaphoreType.DMA],
    )
    grad_k, grad_v = run(
        last_kernel,
        [half, half],
        (key_vec, value_vec, part_k, part_v, near_back, far_back, docs),
        name="last",
        far_outs=(0, 1),
        scratch=[
            pltpu.VMEM((count, columns), BF16),
            pltpu.VMEM((count, columns), BF16),
            pltpu.SemaphoreType.DMA((2 * count // TILE,)),
        ],
    )
    return grad_q, grad_k, grad_v


def solution(mesh):
    in_specs = (
        P("seq", "head"),
        P("seq", "head"),
        P("seq", "head"),
        P("seq", "head"),
        P("head"),
        P("seq"),
        P("seq"),
        P(),
    )
    out_specs = (P("seq", "head"), P("seq", "head"), P("seq", "head"))
    return jax.shard_map(local, mesh=mesh, in_specs=in_specs, out_specs=out_specs, check_vma=False)
```

```python
import jax
import jax.numpy as jnp
from jax import lax
from jax.experimental import pallas as pl
from jax.experimental.pallas import tpu as pltpu
from jax.sharding import PartitionSpec as P

HEAD_DIM = 128
HEADS = 16
NORM_WIDTH = HEADS * HEAD_DIM
EPSILON = 1e-06
TILE = 256
LANES = 128

F32 = jnp.float32
BF16 = jnp.bfloat16


def dot_nt(a, b):
    return lax.dot_general(a, b, (((1,), (1,)), ((), ())), preferred_element_type=F32)


def dot_nn(a, b):
    return lax.dot_general(a, b, (((1,), (0,)), ((), ())), preferred_element_type=F32)


def dot_tn(a, b):
    return lax.dot_general(a, b, (((0,), (0,)), ((), ())), preferred_element_type=F32)


def head_of(h):
    return slice(h * HEAD_DIM, (h + 1) * HEAD_DIM)


def down(rows):
    return jnp.concatenate(
        [
            jnp.broadcast_to(rows[i : i + 1, :], (LANES, LANES)).T
            for i in range(rows.shape[0])
        ]
    )


def across(rows):
    return jnp.concatenate([rows[i : i + 1, :] for i in range(rows.shape[0])], axis=1)


def lifted(columns):
    eye = lax.broadcasted_iota(jnp.int32, (LANES, LANES), 0) == lax.broadcasted_iota(
        jnp.int32, (LANES, LANES), 1
    )
    count = columns.shape[0] // LANES
    return jnp.concatenate(
        [
            jnp.sum(
                jnp.where(eye, columns[i * LANES : (i + 1) * LANES, :], 0.0), axis=0, keepdims=True
            )
            for i in range(count)
        ]
    )


def floats(doc_ref):
    return doc_ref[...].astype(F32)


def first_of(rows):
    return rows[0:1, 0:1]


def last_of(rows):
    return rows[-1:, LANES - 1 : LANES]


def tokens_of(rows, doc):
    hit = jnp.where(rows == doc, 1.0, 0.0)
    return jnp.sum(jnp.sum(hit, axis=0, keepdims=True), axis=1, keepdims=True)


def token_numbers(rows):
    return lax.broadcasted_iota(jnp.int32, (rows.size, LANES), 0).astype(F32)


def in_first(rows):
    return token_numbers(rows) < tokens_of(rows, first_of(rows))


def in_last(rows):
    return token_numbers(rows) >= rows.size - tokens_of(rows, last_of(rows))


def wide(column):
    return jnp.concatenate([column, column], axis=1)


def masked_scores(left, right, doc_left, doc_right, lower):
    raw = dot_nt(left, right)
    width = right.shape[0]
    parts = []
    row = lax.broadcasted_iota(jnp.int32, (TILE, TILE), 0)
    col = lax.broadcasted_iota(jnp.int32, (TILE, TILE), 1)
    on_diagonal = (col <= row) if lower else (row <= col)
    for start in range(0, width, TILE):
        keep = wide(doc_left) == doc_right[:, start : start + TILE]
        if start == (width - TILE if lower else 0):
            keep = keep & on_diagonal
        parts.append(jnp.where(keep, raw[:, start : start + TILE], 0.0).astype(BF16))
    return jnp.concatenate(parts, axis=1) if len(parts) > 1 else parts[0]


def state_kernel(key_hbm, value_hbm, doc_hbm, out_ref, key_ref, value_ref, doc_ref, sems):
    count = key_ref.shape[0]
    halves = [slice(0, count // 2), slice(count // 2, count)]
    copies = [pltpu.make_async_copy(doc_hbm, doc_ref, sems.at[0])]
    for i, part in enumerate(halves):
        copies.append(pltpu.make_async_copy(key_hbm.at[part], key_ref.at[part], sems.at[1 + 2 * i]))
        copies.append(
            pltpu.make_async_copy(value_hbm.at[part], value_ref.at[part], sems.at[2 + 2 * i])
        )
    for copy in copies:
        copy.start()
    copies[0].wait()
    rows = floats(doc_ref)
    doc = last_of(rows)
    keep = in_last(rows)
    totals = [0.0, 0.0]
    for i, part in enumerate(halves):
        copies[1 + 2 * i].wait()
        copies[2 + 2 * i].wait()
        for h in range(2):
            kept = jnp.where(keep[part], key_ref[part, head_of(h)].astype(F32), 0.0).astype(BF16)
            totals[h] = totals[h] + dot_tn(kept, value_ref[part, head_of(h)])
    for h in range(2):
        out_ref[head_of(h), :] = totals[h]
    out_ref[256:264, :] = jnp.broadcast_to(doc + 1.0, (8, LANES))


def pair_kernel(own_ref, got_ref, far_ref, near_ref):
    same = own_ref[256:257, :] == got_ref[256:257, :]
    both = own_ref[0:256, :] + jnp.where(same, got_ref[0:256, :], 0.0)
    near_ref[...] = both
    far_ref[0:256, :] = both
    far_ref[256:264, :] = own_ref[256:264, :]


def window_sum(near_ref, far_ref, got_ref, doc):
    mark = doc + 1.0
    near = jnp.where(got_ref[256:257, :] == mark, near_ref[...], 0.0)
    far = jnp.where(far_ref[256:257, :] == mark, far_ref[0:256, :], 0.0)
    return (near + far).astype(BF16)


def inner_kernel(
    query_ref, key_ref, value_ref, doc_ref, cot_hbm, gain_hbm, lang_hbm, table_hbm,
    inner_ref, up_ref, cot_ref, gain_ref, lang_ref, table_ref, sems,
):
    pairs = ((cot_hbm, cot_ref), (gain_hbm, gain_ref), (lang_hbm, lang_ref), (table_hbm, table_ref))
    copies = [
        pltpu.make_async_copy(hbm, ref, sems.at[i]) for i, (hbm, ref) in enumerate(pairs)
    ]
    for copy in copies:
        copy.start()
    rows = floats(doc_ref)
    doc_down, doc_across = down(rows), across(rows)
    count = query_ref.shape[0]
    weight_down = None
    for top in range(0, count, TILE):
        here, upto = slice(top, top + TILE), slice(0, top + TILE)
        for h in range(2):
            scores = masked_scores(
                query_ref[here, head_of(h)], key_ref[upto, head_of(h)],
                doc_down[here], doc_across[:, upto], True,
            )
            inner_ref[here, head_of(h)] = dot_nn(scores, value_ref[upto, head_of(h)])
        if weight_down is None:
            for copy in copies:
                copy.wait()
            lang = lang_ref[...]
            weight = jnp.zeros(lang.shape, F32)
            for n in range(table_ref.shape[1]):
                weight = weight + jnp.where(lang == n, table_ref[0:1, n : n + 1], 0.0)
            weight_down = down(weight)
        up_ref[here] = cot_ref[here].astype(F32) * wide(weight_down[here]) * gain_ref[...]


def out_kernel(
    query_ref, inner_ref, up_ref, near_ref, far_ref, got_ref, doc_ref,
    out_ref, incoming_ref, sums_ref,
):
    rows = floats(doc_ref)
    first = first_of(rows)
    incoming = window_sum(near_ref, far_ref, got_ref, first)
    incoming_ref[...] = incoming
    keep = in_first(rows)
    squares = mixed = 0.0
    for h in range(2):
        carried = dot_nn(query_ref[:, head_of(h)], incoming[head_of(h)])
        head_out = inner_ref[:, head_of(h)] + jnp.where(keep, carried, 0.0)
        out_ref[:, head_of(h)] = head_out
        squares = squares + head_out * head_out
        mixed = mixed + head_out * up_ref[:, head_of(h)]
    sums = jnp.concatenate(
        [
            lifted(jnp.sum(squares, axis=1, keepdims=True)),
            lifted(jnp.sum(mixed, axis=1, keepdims=True)),
        ]
    )
    for i in range(sums_ref.shape[0]):
        sums_ref[i] = sums


def grad_kernel(sums_ref, out_ref, up_ref, query_ref, doc_ref, grad_ref, state_ref):
    sums = sums_ref[0]
    for i in range(1, sums_ref.shape[0]):
        sums = sums + sums_ref[i]
    half = sums.shape[0] // 2
    inv = lax.rsqrt(sums[:half] / NORM_WIDTH + EPSILON)
    inv_down = down(inv)
    coef_down = down(inv * inv * inv * sums[half:] / NORM_WIDTH)
    rows = floats(doc_ref)
    first = first_of(rows)
    keep = in_first(rows)
    for h in range(2):
        grad = (inv_down * up_ref[:, head_of(h)] - out_ref[:, head_of(h)] * coef_down).astype(BF16)
        grad_ref[:, head_of(h)] = grad
        kept = jnp.where(keep, query_ref[:, head_of(h)].astype(F32), 0.0).astype(BF16)
        state_ref[head_of(h), :] = dot_tn(kept, grad)
    state_ref[256:264, :] = jnp.broadcast_to(first + 1.0, (8, LANES))


def query_kernel(key_ref, value_ref, grad_ref, incoming_ref, doc_ref, out_ref):
    rows = floats(doc_ref)
    first = first_of(rows)
    doc_down, doc_across = down(rows), across(rows)
    count = key_ref.shape[0]
    for top in range(0, count, TILE):
        here, upto = slice(top, top + TILE), slice(0, top + TILE)
        for h in range(2):
            grad = grad_ref[here, head_of(h)]
            scores = masked_scores(
                grad, value_ref[upto, head_of(h)], doc_down[here], doc_across[:, upto], True
            )
            carried = dot_nt(grad, incoming_ref[head_of(h), :])
            total = dot_nn(scores, key_ref[upto, head_of(h)])
            total = total + jnp.where(doc_down[here] == first, carried, 0.0)
            out_ref[here, head_of(h)] = total.astype(BF16)


def key_value_kernel(
    query_ref, key_ref, value_ref, grad_ref, doc_ref, gquery_ref, gkey_ref, gvalue_ref, out_hbm, sem
):
    copy = pltpu.make_async_copy(gquery_ref, out_hbm, sem)
    copy.start()
    rows = floats(doc_ref)
    doc_down, doc_across = down(rows), across(rows)
    count = key_ref.shape[0]
    for top in range(0, count, TILE):
        here, rest = slice(top, top + TILE), slice(top, count)
        for h in range(2):
            query, grad = query_ref[rest, head_of(h)], grad_ref[rest, head_of(h)]
            docs = (doc_down[here], doc_across[:, rest])
            back = masked_scores(value_ref[here, head_of(h)], grad, *docs, False)
            gkey_ref[here, head_of(h)] = dot_nn(back, query)
            scores = masked_scores(key_ref[here, head_of(h)], query, *docs, False)
            gvalue_ref[here, head_of(h)] = dot_nn(scores, grad)
    copy.wait()


def last_kernel(
    key_ref, value_ref, gkey_ref, gvalue_ref, near_ref, far_ref, got_ref, doc_ref,
    okey_hbm, ovalue_hbm, okey_ref, ovalue_ref, sems,
):
    rows = floats(doc_ref)
    last = last_of(rows)
    keep = in_last(rows)
    returning = window_sum(near_ref, far_ref, got_ref, last)
    copies = []
    for top in range(0, key_ref.shape[0], TILE):
        here = slice(top, top + TILE)
        for h in range(2):
            state = returning[head_of(h)]
            key = dot_nt(value_ref[here, head_of(h)], state)
            key = gkey_ref[here, head_of(h)] + jnp.where(keep[here], key, 0.0)
            okey_ref[here, head_of(h)] = key.astype(BF16)
            value = dot_nn(key_ref[here, head_of(h)], state)
            value = gvalue_ref[here, head_of(h)] + jnp.where(keep[here], value, 0.0)
            ovalue_ref[here, head_of(h)] = value.astype(BF16)
        for ref, hbm in ((okey_ref, okey_hbm), (ovalue_ref, ovalue_hbm)):
            copies.append(pltpu.make_async_copy(ref.at[here], hbm.at[here], sems.at[len(copies)]))
            copies[-1].start()
    for copy in copies:
        copy.wait()


def run(kernel, outs, args, flops=0, name=None, far_ins=(), far_outs=(), scratch=(), limit=32):
    shapes = tuple(jax.ShapeDtypeStruct(shape, dtype) for shape, dtype in outs)
    moved = sum(a.size * a.dtype.itemsize for a in (*args, *shapes))
    near, far = pl.BlockSpec(memory_space=pltpu.VMEM), pl.BlockSpec(memory_space=pltpu.HBM)
    got = pl.pallas_call(
        kernel,
        out_shape=shapes,
        in_specs=[far if i in far_ins else near for i in range(len(args))],
        out_specs=tuple(far if i in far_outs else near for i in range(len(shapes))),
        scratch_shapes=scratch,
        compiler_params=pltpu.CompilerParams(vmem_limit_bytes=limit * 1024 * 1024),
        cost_estimate=pl.CostEstimate(flops=flops, bytes_accessed=moved, transcendentals=0),
        name=name,
    )(
        *(
            pltpu.with_memory_space_constraint(a, pltpu.HBM) if i in far_ins else a
            for i, a in enumerate(args)
        )
    )
    return got[0] if len(outs) == 1 else got


def shift(payload, step):
    count = lax.axis_size("seq")
    pairs = [(i, i + step) for i in range(count) if 0 <= i + step < count]
    return lax.ppermute(payload, "seq", pairs)


def local(query_vec, key_vec, value_vec, cotangent, norm_gain, doc_ids, lang_ids, loss_table):
    count, columns = query_vec.shape
    docs = doc_ids.reshape(-1, LANES)
    langs = lang_ids.reshape(-1, LANES)
    square = 2 * columns * count * count
    packed = ((columns + 8, LANES), F32)
    plain = ((columns, LANES), F32)
    full = ((count, columns), F32)
    half = ((count, columns), BF16)

    own, key_vec, value_vec = run(
        state_kernel,
        [packed, half, half],
        (key_vec, value_vec, docs),
        name="state",
        far_ins=(0, 1, 2),
        scratch=[
            pltpu.VMEM(docs.shape, jnp.int32),
            pltpu.SemaphoreType.DMA((5,)),
        ],
    )
    got = shift(own, 1)
    inner, up = run(
        inner_kernel,
        [full, full],
        (
            query_vec, key_vec, value_vec, docs, cotangent, norm_gain[None, :], langs,
            loss_table[None, :],
        ),
        flops=2 * square,
        name="inner",
        far_ins=(4, 5, 6, 7),
        scratch=[
            pltpu.VMEM((count, columns), BF16),
            pltpu.VMEM((1, columns), F32),
            pltpu.VMEM(langs.shape, jnp.int32),
            pltpu.VMEM((1, loss_table.shape[0]), F32),
            pltpu.SemaphoreType.DMA((4,)),
        ],
    )
    pair = run(pair_kernel, [packed, plain], (own, got), name="pair")
    far, near = shift(pair[0], 3), shift(pair[1], 1)
    heads = lax.axis_size("head")
    head_out, incoming, sums = run(
        out_kernel,
        [full, ((columns, LANES), BF16), ((heads, 2 * count // LANES, LANES), F32)],
        (query_vec, inner, up, near, far, got, docs),
        name="out",
    )
    sums = lax.all_to_all(sums, "head", 0, 0)
    grad, own_back = run(
        grad_kernel, [half, packed], (sums, head_out, up, query_vec, docs), name="grad"
    )
    got_back = shift(own_back, -1)
    part_q = run(
        query_kernel,
        [half],
        (key_vec, value_vec, grad, incoming, docs),
        flops=2 * square,
        name="query",
    )
    pair_back = run(
        lambda own_ref, got_ref, _, *outs: pair_kernel(own_ref, got_ref, *outs),
        [packed, plain],
        (own_back, got_back, part_q),
        name="pair_back",
    )
    far_back, near_back = shift(pair_back[0], -3), shift(pair_back[1], -1)
    part_k, part_v, grad_q = run(
        key_value_kernel,
        [full, full, half],
        (query_vec, key_vec, value_vec, grad, docs, part_q),
        flops=4 * square,
        name="key_value",
        far_outs=(2,),
        scratch=[pltpu.SemaphoreType.DMA],
    )
    grad_k, grad_v = run(
        last_kernel,
        [half, half],
        (key_vec, value_vec, part_k, part_v, near_back, far_back, got_back, docs),
        name="last",
        far_outs=(0, 1),
        scratch=[
            pltpu.VMEM((count, columns), BF16),
            pltpu.VMEM((count, columns), BF16),
            pltpu.SemaphoreType.DMA((2 * count // TILE,)),
        ],
    )
    return grad_q, grad_k, grad_v


def solution(mesh):
    in_specs = (
        P("seq", "head"),
        P("seq", "head"),
        P("seq", "head"),
        P("seq", "head"),
        P("head"),
        P("seq"),
        P("seq"),
        P(),
    )
    out_specs = (P("seq", "head"), P("seq", "head"), P("seq", "head"))
    return jax.shard_map(local, mesh=mesh, in_specs=in_specs, out_specs=out_specs, check_vma=False)
```
